256 devices in a mesh: row: 8 (over z_hi, y), col: 32 (over z_lo, x, core).
Axes of the slice: x: 4, y: 4, z: 8 (z_hi: 2, z_lo: 4; z = z_hi * 4 + z_lo), core: 2. Of those that a mesh axis runs over, the one named last changes fastest.
Arguments:
- inputs: bfloat16 [1024, 12288], P('col', 'row'), may hold values from -6 to 6
- weight: bfloat16 [12288, 49152], P('row', 'col'), may hold values from -0.0546875 to 0.0546875
- hidden_bias: float32 [49152], P('col'), may hold values from -3 to 3
- act_cotangent: bfloat16 [1024, 49152], P('row', 'col'), may hold values from -6 to 6
Outputs:
- activated: bfloat16 [1024, 49152], P('row', 'col')
- input_grad: bfloat16 [1024, 12288], P('col', 'row')
- weight_grad: bfloat16 [12288, 49152], P('row', 'col')
- bias_grad: float32 [49152], P('col')
The draws below stay inside these ranges and needn't reach their ends.
All inputs are finite; a program needn't handle non-finite values.
Results may differ from the reference program's by a relative error of at most 0.007.
Values may be sent and summed in bfloat16 or wider, within the bound.
A program may use at most 128 MiB of HBM per device.

```python
import math
import jax
import jax.numpy as jnp
from jax import lax

D = 12288
FF = 49152
TOKENS = 1024


def strengthened(drawn, key, source, target, shards_of, factor):
    def block_of(dim):
        return (jnp.arange(drawn.shape[dim]) // (drawn.shape[dim] // shards_of)).reshape((-1,) + (1,) * (drawn.ndim - 1 - dim))

    near = jax.random.permutation(key, shards_of)[block_of(target)]
    second = (block_of(target) + shards_of // 2) % shards_of
    return jnp.where((block_of(source) == near) | (block_of(source) == second), factor * drawn, drawn)


def block_levels(key, shape, split, smallest, largest):
    def one(dim, shards_of):
        draws = jax.random.uniform(jax.random.fold_in(jax.random.fold_in(key, 6), dim), (shards_of,), jnp.float32, smallest / len(split), largest / len(split))
        return jnp.repeat(jnp.exp(draws), shape[dim] // shards_of).reshape((-1,) + (1,) * (len(shape) - dim - 1))

    gain = one(*split[0])
    for cut in split[1:]:
        gain = gain * one(*cut)
    return gain


def bell_draw(own_key, dims, scale, bound, shards=(), dtype=jnp.bfloat16):
    result = scale * jax.random.normal(own_key, dims, jnp.float32)
    if shards:
        result = result * block_levels(own_key, dims, shards, -0.22, 0.18)
    return jnp.clip(result, -bound, bound).astype(dtype)


def gaussian_with(key, dims, scale, most, cuts, heavy, kind=jnp.bfloat16):
    result = scale * jax.random.normal(key, dims, jnp.float32)
    if cuts:
        result = result * block_levels(key, dims, cuts, -0.22, 0.18)
    return jnp.clip(strengthened(result, jax.random.fold_in(key, 3), *heavy), -most, most).astype(kind)


def setup_inputs(seed: int = 0) -> dict:
    streams_of = jax.random.split(jax.random.key(seed), 5)
    return {
        "inputs": gaussian_with(streams_of[0], (TOKENS, D), 1.0, 6.0, ((0, 32), (1, 8)), (1, 0, 32, 2.75)),
        "weight": bell_draw(streams_of[1], (D, FF), D ** -0.5, 0.0546875, ((0, 8), (1, 32))),
        "hidden_bias": bell_draw(streams_of[2], (FF,), 0.5, 3.0, ((0, 32),), jnp.float32),
        "act_cotangent": gaussian_with(streams_of[3], (TOKENS, FF), 1.0, 6.0, ((0, 8), (1, 32)), (1, 0, 32, 2.75)),
    }


gelu_const = math.sqrt(2.0 / math.pi)

def gelu_value(value):
    inner = jnp.tanh(gelu_const * (value + 0.044715 * value * value * value))
    return 0.5 * value * (1.0 + inner)

def gelu_slope(value):
    inner = jnp.tanh(gelu_const * (value + 0.044715 * value * value * value))
    return 0.5 * (1.0 + inner) + 0.5 * value * (1.0 - inner * inner) * gelu_const * (1.0 + 3.0 * 0.044715 * value * value)

def reference(inputs, weight, hidden_bias, act_cotangent):
    hidden = jnp.dot(inputs, weight, preferred_element_type=jnp.float32) + hidden_bias[None, :]
    activated = gelu_value(hidden).astype(jnp.bfloat16)
    hidden_cotangent = (act_cotangent.astype(jnp.float32) * gelu_slope(hidden)).astype(jnp.bfloat16)
    bias_grad = lax.optimization_barrier(jnp.sum(hidden_cotangent.astype(jnp.float32), axis=0))
    weight_grad = lax.dot_general(inputs, hidden_cotangent, (((0,), (0,)), ((), ())), preferred_element_type=jnp.float32).astype(jnp.bfloat16)
    input_grad = lax.dot_general(hidden_cotangent, weight, (((1,), (1,)), ((), ())), preferred_element_type=jnp.float32).astype(jnp.bfloat16)
    return (activated, input_grad, weight_grad, bias_grad)
```

```python
import math

import jax
import jax.numpy as jnp
from jax import lax
from jax.experimental import pallas as pl
from jax.experimental.pallas import tpu as pltpu
from jax.sharding import PartitionSpec as P

gelu_const = math.sqrt(2.0 / math.pi)
BF = jnp.bfloat16
F32 = jnp.float32
MESH = pl.DeviceIdType.MESH

HALVES = 2
CH = 3
WIDTH = 1536
F = WIDTH // CH
UNITS = HALVES * CH


def dot_nn(a, b):
    return lax.dot_general(a, b, (((1,), (0,)), ((), ())), preferred_element_type=F32)


def dot_nt(a, b):
    return lax.dot_general(a, b, (((1,), (1,)), ((), ())), preferred_element_type=F32)


def dot_tn(a, b):
    return lax.dot_general(a, b, (((0,), (0,)), ((), ())), preferred_element_type=F32)


def kernel(
    x_hbm, w_hbm, bias_ref, ct_hbm,
    act_hbm, ig_ref, wg_hbm, bg_ref,
    X, W, CT, ACT, PH, RA, RB, RC, CB, ZS, ZR, OWN, COT,
    IGB, RK, S, XA, XB, XC, XM, T, ZT, WG,
    loc, wgsem, actsem,
    az, ax, af, ak, ry, rz, gz, gy, gf, ck, cx, cz,
    saz, sax, saf, sak, sry, srz, sgz, sgy, sgf, sck, scx, scz,
):
    r = lax.axis_index("row")
    c = lax.axis_index("col")
    zh, y = r // 4, r % 4
    zl, x, k = c // 8, (c // 2) % 4, c % 2

    yp = (zh * 4 + (y + 1) % 4, c)
    ym = (zh * 4 + (y + 3) % 4, c)
    zpart = ((1 - zh) * 4 + y, c)
    xp = (r, zl * 8 + ((x + 1) % 4) * 2 + k)
    xm = (r, zl * 8 + ((x + 3) % 4) * 2 + k)
    core = (r, zl * 8 + x * 2 + (1 - k))
    zls = [zl, zl + 1 - 2 * (zl % 2), (zl + 2) % 4, 3 - zl]
    zpeer = [None] + [(r, zls[m] * 8 + x * 2 + k) for m in (1, 2, 3)]
    xpeer = (xp, xm)

    started = []

    def remote(src, dst, ssem, rsem, dev):
        return pltpu.make_async_remote_copy(
            src_ref=src, dst_ref=dst, send_sem=ssem, recv_sem=rsem, device_id=dev, device_id_type=MESH
        )

    def send(*args):
        copy = remote(*args)
        copy.start()
        started.append(copy)

    def arrived(dst, rsem, ssem):
        remote(dst, dst, ssem, rsem, core).wait_recv()

    cp_x = [pltpu.make_async_copy(x_hbm.at[h], X.at[h, zl, x, k], loc.at[h]) for h in range(HALVES)]
    cp_w = pltpu.make_async_copy(w_hbm, W, loc.at[2])
    cp_ct = pltpu.make_async_copy(ct_hbm, CT, loc.at[3])
    for cp in cp_x:
        cp.start()
    cp_w.start()
    cp_ct.start()
    barrier = pltpu.get_barrier_semaphore()
    peers = [yp, ym, zpart, xp, xm, core] + zpeer[1:]
    for p in peers:
        pl.semaphore_signal(barrier, inc=1, device_id=p, device_id_type=MESH)
    pl.semaphore_wait(barrier, len(peers))
    for cp in cp_x:
        cp.wait()

    def ag_start(h):
        own = X.at[h, zl, x, k]
        for m in (1, 2, 3):
            send(own, own, saz.at[h, m - 1], az.at[h, m - 1], zpeer[m])
        for d in range(2):
            send(own, own, sax.at[h, d, 0], ax.at[h, d, 0], xpeer[d])

    def ag_z(h):
        for m in (1, 2, 3):
            blk = X.at[h, zls[m], x, k]
            arrived(blk, az.at[h, m - 1], saz.at[h, m - 1])
            for d in range(2):
                send(blk, blk, sax.at[h, d, m], ax.at[h, d, m], xpeer[d])
        col = X.at[h, :, x, k]
        send(col, col, sak.at[h, 0], ak.at[h, 0], core)

    def ag_f(h):
        for m in range(4):
            for d in range(2):
                blk = X.at[h, zls[m], (x + 3 - 2 * d) % 4, k]
                arrived(blk, ax.at[h, d, m], sax.at[h, d, m])
                if d == m // 2:
                    send(blk, blk, saf.at[h, m], af.at[h, m], xpeer[d])
        for d in range(2):
            col = X.at[h, :, (x + 3 - 2 * d) % 4, k]
            send(col, col, sak.at[h, 1 + d], ak.at[h, 1 + d], core)

    def ag_k(h):
        for m in range(4):
            blk = X.at[h, zls[m], (x + 2) % 4, k]
            arrived(blk, af.at[h, m], saf.at[h, m])
        col = X.at[h, :, (x + 2) % 4, k]
        send(col, col, sak.at[h, 3], ak.at[h, 3], core)

    def ag_done(h):
        for i, xx in enumerate((x, (x + 3) % 4, (x + 1) % 4, (x + 2) % 4)):
            col = X.at[h, :, xx, 1 - k]
            arrived(col, ak.at[h, i], sak.at[h, i])

    def cols(j):
        return pl.ds(j * F, F)

    def m1(u):
        h, j = divmod(u, CH)
        js = cols(j)
        part = dot_nn(X[h].reshape(512, WIDTH), W[:, js])
        PH[h, :, :, js] = part.astype(BF).reshape(8, 64, F)
        y1, y2, y3 = (y + 1) % 4, (y + 2) % 4, (y + 3) % 4
        send(PH.at[h, y2, :, js], RA.at[h, 0, :, js], sry.at[u, 0], ry.at[u, 0], yp)
        send(PH.at[h, y2 + 4, :, js], RA.at[h, 1, :, js], sry.at[u, 1], ry.at[u, 1], ym)
        send(PH.at[h, y1 + 4, :, js], RB.at[h, 1, :, js], sry.at[u, 2], ry.at[u, 2], yp)
        send(PH.at[h, y3, :, js], RB.at[h, 0, :, js], sry.at[u, 3], ry.at[u, 3], ym)

    def r1(u):
        h, j = divmod(u, CH)
        js = cols(j)
        for s in range(2):
            arrived(RA.at[h, s, :, js], ry.at[u, s], sry.at[u, s])
            nxt = (y + 1 + 2 * s) % 4 + 4 * s
            CB[h, s, :, js] = (PH[h, nxt, :, js].astype(F32) + RA[h, s, :, js].astype(F32)).astype(BF)
            send(CB.at[h, s, :, js], RC.at[h, s, :, js], sry.at[u, 4 + s], ry.at[u, 4 + s], (yp, ym)[s])

    def r2(u):
        h, j = divmod(u, CH)
        js = cols(j)
        for i, buf in ((2, RB.at[h, 1]), (3, RB.at[h, 0]), (4, RC.at[h, 0]), (5, RC.at[h, 1])):
            arrived(buf.at[:, js], ry.at[u, i], sry.at[u, i])

        def total(s):
            return (
                PH[h, y + 4 * s, :, js].astype(F32)
                + RB[h, s, :, js].astype(F32)
                + RC[h, s, :, js].astype(F32)
            )

        ZS[h, :, js] = total(1 - zh).astype(BF)
        send(ZS.at[h, :, js], ZR.at[h, :, js], srz.at[u], rz.at[u], zpart)
        OWN[h, :, js] = total(zh)

    def g(u):
        h, j = divmod(u, CH)
        js = cols(j)
        arrived(ZR.at[h, :, js], rz.at[u], srz.at[u])
        v = OWN[h, :, js] + ZR[h, :, js].astype(F32) + bias_ref[:, js]
        sq = v * v
        t = jnp.tanh(gelu_const * v * (1.0 + 0.044715 * sq))
        half = 0.5 * (1.0 + t)
        ACT[:, h, :, js] = (v * half).astype(BF).reshape(4, 16, F)
        slope = half + 0.5 * v * (1.0 - t * t) * gelu_const * (1.0 + 3.0 * 0.044715 * sq)
        ct = CT[:, h, :, js].reshape(64, F).astype(F32)
        COT[h, r, :, js] = (ct * slope).astype(BF)
        own = COT.at[h, r, :, js]
        send(own, own, sgz.at[u], gz.at[u], zpart)
        for d in range(2):
            send(own, own, sgy.at[u, d, zh], gy.at[u, d, zh], (yp, ym)[d])
        pltpu.make_async_copy(
            ACT.at[:, h, :, js], act_hbm.at[:, h, :, js], actsem.at[u]
        ).start()

    def yo(u):
        h, j = divmod(u, CH)
        js = cols(j)
        oth = COT.at[h, (1 - zh) * 4 + y, :, js]
        arrived(oth, gz.at[u], sgz.at[u])
        for d in range(2):
            send(oth, oth, sgy.at[u, d, 1 - zh], gy.at[u, d, 1 - zh], (yp, ym)[d])

    def fw(u, s):
        h, j = divmod(u, CH)
        js = cols(j)
        blk = COT.at[h, (y + 3 + 2 * s) % 4 + 4 * s, :, js]
        arrived(blk, gy.at[u, s, s], sgy.at[u, s, s])
        send(blk, blk, sgf.at[u, s], gf.at[u, s], (zh * 4 + (y + 1 + 2 * s) % 4, c))

    def fwo(u):
        fw(u, zh)

    def fwp(u):
        fw(u, 1 - zh)

    def gd(u):
        h, j = divmod(u, CH)
        js = cols(j)
        for s in range(2):
            d = 1 - s
            arrived(COT.at[h, (y + 3 - 2 * d) % 4 + 4 * s, :, js], gy.at[u, d, s], sgy.at[u, d, s])
            arrived(COT.at[h, (y + 2) % 4 + 4 * s, :, js], gf.at[u, s], sgf.at[u, s])

    def m3(h, n):
        ns = cols(n)
        part = dot_nt(COT[h].reshape(512, WIDTH), W[ns, :])
        IGB[h, :, :, :, :, ns] = part.astype(BF).reshape(4, 4, 2, 16, F)
        send(IGB.at[h, :, :, 1 - k, :, ns], RK.at[h, :, :, :, ns], sck.at[h, n], ck.at[h, n], core)

    def k1(h, n):
        ns = cols(n)
        arrived(RK.at[h, :, :, :, ns], ck.at[h, n], sck.at[h, n])
        S[h, :, :, :, ns] = (
            IGB[h, :, :, k, :, ns].astype(F32) + RK[h, :, :, :, ns].astype(F32)
        ).astype(BF)
        x1, x2, x3 = (x + 1) % 4, (x + 2) % 4, (x + 3) % 4
        lo, hi = pl.ds(0, 2), pl.ds(2, 2)
        send(S.at[h, lo, x2, :, ns], XA.at[h, 0, :, :, ns], scx.at[h, n, 0], cx.at[h, n, 0], xp)
        send(S.at[h, hi, x2, :, ns], XA.at[h, 1, :, :, ns], scx.at[h, n, 1], cx.at[h, n, 1], xm)
        send(S.at[h, hi, x1, :, ns], XB.at[h, 1, :, :, ns], scx.at[h, n, 2], cx.at[h, n, 2], xp)
        send(S.at[h, lo, x3, :, ns], XB.at[h, 0, :, :, ns], scx.at[h, n, 3], cx.at[h, n, 3], xm)

    def k2(h, n):
        ns = cols(n)
        for s in range(2):
            arrived(XA.at[h, s, :, :, ns], cx.at[h, n, s], scx.at[h, n, s])
            pair = pl.ds(2 * s, 2)
            XM[h, s, :, :, ns] = (
                S[h, pair, (x + 1 + 2 * s) % 4, :, ns].astype(F32) + XA[h, s, :, :, ns].astype(F32)
            ).astype(BF)
            send(
                XM.at[h, s, :, :, ns], XC.at[h, s, :, :, ns],
                scx.at[h, n, 4 + s], cx.at[h, n, 4 + s], xpeer[s],
            )

    def k3(h, n):
        ns = cols(n)
        for i, buf in ((2, XB.at[h, 1]), (3, XB.at[h, 0]), (4, XC.at[h, 0]), (5, XC.at[h, 1])):
            arrived(buf.at[:, :, ns], cx.at[h, n, i], scx.at[h, n, i])
        for s in range(2):
            pair = pl.ds(2 * s, 2)
            T[h, pair, :, ns] = (
                S[h, pair, x, :, ns].astype(F32)
                + XB[h, s, :, :, ns].astype(F32)
                + XC[h, s, :, :, ns].astype(F32)
            ).astype(BF)
        for m in (1, 2, 3):
            send(
                T.at[h, zls[m], :, ns], ZT.at[h, m - 1, :, ns],
                scz.at[h, n, m - 1], cz.at[h, n, m - 1], zpeer[m],
            )

    def k4(h, n):
        ns = cols(n)
        total = T[h, zl, :, ns].astype(F32)
        for m in (1, 2, 3):
            arrived(ZT.at[h, m - 1, :, ns], cz.at[h, n, m - 1], scz.at[h, n, m - 1])
            total = total + ZT[h, m - 1, :, ns].astype(F32)
        ig_ref[h, :, ns] = total.astype(BF)

    def m2(m, j):
        ms, js = cols(m), cols(j)
        a = X[:, :, :, :, :, ms].reshape(1024, F)
        b = COT[:, :, :, js].reshape(1024, F)
        WG[ms, js] = dot_tn(a, b).astype(BF)

    def m2_out(m):
        pltpu.make_async_copy(WG.at[cols(m)], wg_hbm.at[cols(m)], wgsem.at[m]).start()

    def bg(j):
        js = cols(j)
        bg_ref[:, js] = jnp.sum(COT[:, :, :, js].astype(F32).reshape(1024, F), axis=0, keepdims=True)

    ag_start(0)
    ag_z(0)
    ag_start(1)
    ag_f(0)
    ag_k(0)
    ag_done(0)
    cp_w.wait()
    cp_ct.wait()
    m1(0)
    ag_z(1)
    m1(1)
    r1(0)
    ag_f(1)
    m1(2)
    r1(1)
    r2(0)
    ag_k(1)
    r1(2)
    r2(1)
    ag_done(1)
    m1(3)
    r2(2)
    m1(4)
    r1(3)
    g(0)
    m1(5)
    r1(4)
    r2(3)
    g(1)
    yo(0)
    fwo(0)
    r1(5)
    r2(4)
    g(2)
    yo(1)
    fwo(1)
    fwp(0)
    r2(5)
    g(3)
    yo(2)
    fwo(2)
    fwp(1)
    g(4)
    yo(3)
    fwo(3)
    fwp(2)
    gd(0)
    gd(1)
    gd(2)
    for n in range(CH):
        m3(0, n)
    k1(0, 0)
    g(5)
    yo(4)
    fwo(4)
    fwp(3)
    k1(0, 1)
    k1(0, 2)
    k2(0, 0)
    yo(5)
    fwo(5)
    fwp(4)
    k2(0, 1)
    k2(0, 2)
    k3(0, 0)
    fwp(5)
    k3(0, 1)
    k3(0, 2)
    gd(3)
    gd(4)
    gd(5)
    m3(1, 0)
    m3(1, 1)
    k1(1, 0)
    m3(1, 2)
    k1(1, 1)
    k1(1, 2)
    for n in range(CH):
        k4(0, n)
    bg(0)
    k2(1, 0)
    bg(1)
    k2(1, 1)
    bg(2)
    k2(1, 2)
    m2(0, 0)
    m2(0, 1)
    k3(1, 0)
    m2(0, 2)
    m2_out(0)
    k3(1, 1)
    m2(1, 0)
    k3(1, 2)
    m2(1, 1)
    m2(1, 2)
    m2_out(1)
    m2(2, 0)
    m2(2, 1)
    m2(2, 2)
    m2_out(2)
    for n in range(CH):
        k4(1, n)

    for copy in started:
        copy.wait_send()
    for u in range(UNITS):
        h, j = divmod(u, CH)
        pltpu.make_async_copy(ACT.at[:, h, :, cols(j)], act_hbm.at[:, h, :, cols(j)], actsem.at[u]).wait()
    for m in range(CH):
        pltpu.make_async_copy(WG.at[cols(m)], wg_hbm.at[cols(m)], wgsem.at[m]).wait()


def local(inputs, weight, hidden_bias, act_cotangent):
    dma = pltpu.SemaphoreType.DMA
    sems = [
        (2, 3), (2, 2, 4), (2, 4), (2, 4),
        (UNITS, 6), (UNITS,), (UNITS,), (UNITS, 2, 2), (UNITS, 2),
        (2, CH), (2, CH, 6), (2, CH, 3),
    ]
    scratch = [
        pltpu.VMEM((2, 4, 4, 2, 16, WIDTH), BF),
        pltpu.VMEM((WIDTH, WIDTH), BF),
        pltpu.VMEM((4, 2, 16, WIDTH), BF),
        pltpu.VMEM((4, 2, 16, WIDTH), BF),
        pltpu.VMEM((2, 8, 64, WIDTH), BF),
        pltpu.VMEM((2, 2, 64, WIDTH), BF),
        pltpu.VMEM((2, 2, 64, WIDTH), BF),
        pltpu.VMEM((2, 2, 64, WIDTH), BF),
        pltpu.VMEM((2, 2, 64, WIDTH), BF),
        pltpu.VMEM((2, 64, WIDTH), BF),
        pltpu.VMEM((2, 64, WIDTH), BF),
        pltpu.VMEM((2, 64, WIDTH), F32),
        pltpu.VMEM((2, 8, 64, WIDTH), BF),
        pltpu.VMEM((2, 4, 4, 2, 16, WIDTH), BF),
        pltpu.VMEM((2, 4, 4, 16, WIDTH), BF),
        pltpu.VMEM((2, 4, 4, 16, WIDTH), BF),
        pltpu.VMEM((2, 2, 2, 16, WIDTH), BF),
        pltpu.VMEM((2, 2, 2, 16, WIDTH), BF),
        pltpu.VMEM((2, 2, 2, 16, WIDTH), BF),
        pltpu.VMEM((2, 2, 2, 16, WIDTH), BF),
        pltpu.VMEM((2, 4, 16, WIDTH), BF),
        pltpu.VMEM((2, 3, 16, WIDTH), BF),
        pltpu.VMEM((WIDTH, WIDTH), BF),
        dma((4,)), dma((CH,)), dma((UNITS,)),
    ] + [dma(s) for s in sems + sems]
    hbm = pl.BlockSpec(memory_space=pl.ANY)
    vmem = pl.BlockSpec(memory_space=pltpu.VMEM)
    act, ig, wg, bgr = pl.pallas_call(
        kernel,
        out_shape=(
            jax.ShapeDtypeStruct((4, 2, 16, WIDTH), BF),
            jax.ShapeDtypeStruct((2, 16, WIDTH), BF),
            jax.ShapeDtypeStruct((WIDTH, WIDTH), BF),
            jax.ShapeDtypeStruct((1, WIDTH), F32),
        ),
        in_specs=[hbm, hbm, vmem, hbm],
        out_specs=(hbm, vmem, hbm, vmem),
        scratch_shapes=scratch,
        compiler_params=pltpu.CompilerParams(
            collective_id=0, has_side_effects=True, vmem_limit_bytes=56 << 20
        ),
        name="ffn",
    )(
        inputs.reshape(2, 16, WIDTH),
        weight,
        hidden_bias.reshape(1, WIDTH),
        act_cotangent.reshape(4, 2, 16, WIDTH),
    )
    return act.reshape(128, WIDTH), ig.reshape(32, WIDTH), wg, bgr.reshape(WIDTH)


def solution(mesh):
    in_specs = (P("col", "row"), P("row", "col"), P("col"), P("row", "col"))
    out_specs = (P("row", "col"), P("col", "row"), P("row", "col"), P("col"))
    return jax.shard_map(local, mesh=mesh, in_specs=in_specs, out_specs=out_specs, check_vma=False)
```

```python
import math

import jax
import jax.numpy as jnp
from jax import lax
from jax.experimental import pallas as pl
from jax.experimental.pallas import tpu as pltpu
from jax.sharding import PartitionSpec as P

gelu_const = math.sqrt(2.0 / math.pi)
BF = jnp.bfloat16
F32 = jnp.float32
MESH = pl.DeviceIdType.MESH

WIDTH = 1536
Q = 4
J = 2
F = WIDTH // J
F2 = F // 2
UNITS = Q * J
NS = (1, 1, 2, 2)
NMAX = max(NS)


def dot_nn(a, b):
    return lax.dot_general(a, b, (((1,), (0,)), ((), ())), preferred_element_type=F32)


def dot_nt(a, b):
    return lax.dot_general(a, b, (((1,), (1,)), ((), ())), preferred_element_type=F32)


def dot_tn(a, b):
    return lax.dot_general(a, b, (((0,), (0,)), ((), ())), preferred_element_type=F32)


ORDER = (
    ("ag_start", 0), ("ag_start", 1), ("ag_z", 0), ("ag_z", 1), ("ag_f", 0), ("ag_z", 2), ("ag_f", 1),
    ("ag_k", 0), ("ag_z", 3), ("ag_done", 0), ("wload",), ("m1", 1), ("ag_k", 1), ("ag_f", 2),
    ("m1", 0), ("ag_done", 1), ("ag_f", 3), ("m1", 3), ("r1", 0), ("ag_k", 2), ("ag_k", 3),
    ("r1", 3), ("m1", 2), ("r1", 1), ("r2", 0), ("ag_done", 2), ("ag_done", 3), ("r2", 3),
    ("r1", 2), ("m1", 4), ("r2", 1), ("r2", 2), ("m1", 7), ("m1", 6), ("go", 0),
    ("m1", 5), ("go", 3), ("r1", 6), ("r1", 4), ("r1", 7), ("go", 2), ("go", 1),
    ("r2", 6), ("r1", 5), ("r2", 4), ("fo", 0), ("r2", 7), ("gn", 0), ("fo", 3),
    ("gn", 3), ("gn", 2), ("fn", 3), ("fo", 2), ("fo", 1), ("r2", 5), ("go", 4),
    ("fn", 2), ("gn", 1), ("gd", 3), ("go", 6), ("fn", 0), ("fn", 1), ("go", 5),
    ("gd", 2), ("go", 7), ("act_out",), ("gd", 0), ("m3", 1, 0), ("gd", 1), ("gn", 6),
    ("m3", 0, 0), ("fo", 5), ("fo", 6), ("k1", 1, 0), ("gn", 4), ("fo", 4), ("k1", 0, 0),
    ("gn", 7), ("k2", 1, 0), ("fo", 7), ("gn", 5), ("fn", 6), ("fn", 4), ("fn", 7),
    ("k2", 0, 0), ("k3", 1, 0), ("fn", 5), ("gd", 6), ("gd", 4), ("gd", 7), ("m3", 3, 1),
    ("m3", 3, 0), ("gd", 5), ("m3", 2, 1), ("k1", 3, 1), ("m3", 2, 0), ("k1", 3, 0), ("k1", 2, 1),
    ("m2", 1, 2), ("m2", 2, 2), ("k2", 3, 1), ("k1", 2, 0), ("k2", 3, 0), ("m2", 0, 2), ("m2", 1, 0),
    ("k2", 2, 1), ("k3", 0, 0), ("k2", 2, 0), ("k3", 3, 1), ("bg", 0), ("k3", 3, 0), ("k3", 2, 1),
    ("m2", 1, 1), ("m2_out", 1), ("bg", 1), ("k3", 2, 0), ("m2", 0, 1), ("m2", 0, 0), ("m2_out", 0),
    ("m2", 2, 0), ("m2", 2, 1), ("m2_out", 2), ("k4", 0), ("k4", 1),
)


def kernel(
    x_hbm, w_hbm, bias_ref, ct_hbm,
    act_hbm, ig_ref, wg_hbm, bg_ref,
    X, W, CT, ACT, PH, RA, RB, RC, CB, ZS, ZR, OWN, COT,
    IGB, RK, S, XA, XB, XC, XM, T, ZT, WG,
    loc, wgsem, actsem,
    az, ax, af, ak, ry, rz, gz, gy, gf, ck, cx, cz,
    saz, sax, saf, sak, sry, srz, sgz, sgy, sgf, sck, scx, scz,
):
    r = lax.axis_index("row")
    c = lax.axis_index("col")
    zh, y = r // 4, r % 4
    zl, x, k = c // 8, (c // 2) % 4, c % 2

    yp = (zh * 4 + (y + 1) % 4, c)
    ym = (zh * 4 + (y + 3) % 4, c)
    ypeer = (yp, ym)
    zpart = ((1 - zh) * 4 + y, c)
    xp = (r, zl * 8 + ((x + 1) % 4) * 2 + k)
    xm = (r, zl * 8 + ((x + 3) % 4) * 2 + k)
    xpeer = (xp, xm)
    core = (r, zl * 8 + x * 2 + (1 - k))
    zls = [zl, zl + 1 - 2 * (zl % 2), (zl + 2) % 4, 3 - zl]
    zpeer = [None] + [(r, zls[m] * 8 + x * 2 + k) for m in (1, 2, 3)]

    ss = [zl // 2, 1 - zl // 2] * 2
    owner = [zh == ss[q] for q in range(Q)]
    other = [zh != ss[q] for q in range(Q)]

    started = []

    def remote(src, dst, ssem, rsem, dev):
        return pltpu.make_async_remote_copy(
            src_ref=src, dst_ref=dst, send_sem=ssem, recv_sem=rsem, device_id=dev, device_id_type=MESH
        )

    def send(*args):
        copy = remote(*args)
        copy.start()
        started.append(copy)

    def arrived(dst, rsem, ssem):
        remote(dst, dst, ssem, rsem, core).wait_recv()

    cp_x = [pltpu.make_async_copy(x_hbm.at[h], X.at[h, zl, x, k], loc.at[h]) for h in range(2)]
    cp_w = pltpu.make_async_copy(w_hbm, W, loc.at[2])
    cp_ct = pltpu.make_async_copy(ct_hbm, CT, loc.at[3])
    for cp in cp_x:
        cp.start()
    cp_w.start()
    cp_ct.start()
    barrier = pltpu.get_barrier_semaphore()
    peers = [yp, ym, zpart, xp, xm, core] + zpeer[1:]
    for p in peers:
        pl.semaphore_signal(barrier, inc=1, device_id=p, device_id_type=MESH)
    pl.semaphore_wait(barrier, len(peers))
    for cp in cp_x:
        cp.wait()

    def wload():
        cp_w.wait()
        cp_ct.wait()

    def ag_start(h):
        own = X.at[h, zl, x, k]
        send(own, own, saz.at[h, 0], az.at[h, 0], zpeer[1])
        for d in range(2):
            send(own, own, sax.at[h, d, 0], ax.at[h, d, 0], xpeer[d])
        for m in (2, 3):
            send(own, own, saz.at[h, m - 1], az.at[h, m - 1], zpeer[m])

    def planes(q):
        return pl.ds(2 * ss[q], 2)

    def ag_z(q):
        h, p = divmod(q, 2)
        for m in ((1,), (2, 3))[p]:
            blk = X.at[h, zls[m], x, k]
            arrived(blk, az.at[h, m - 1], saz.at[h, m - 1])
            for d in range(2):
                send(blk, blk, sax.at[h, d, m], ax.at[h, d, m], xpeer[d])
        col = X.at[h, planes(q), x, k]
        send(col, col, sak.at[q, 0], ak.at[q, 0], core)

    def ag_f(q):
        h, p = divmod(q, 2)
        for m in (2 * p, 2 * p + 1):
            for d in (m % 2, 1 - m % 2):
                blk = X.at[h, zls[m], (x + 3 - 2 * d) % 4, k]
                arrived(blk, ax.at[h, d, m], sax.at[h, d, m])
                if d == m % 2:
                    send(blk, blk, saf.at[h, m], af.at[h, m], xpeer[d])
        for d in range(2):
            col = X.at[h, planes(q), (x + 3 - 2 * d) % 4, k]
            send(col, col, sak.at[q, 1 + d], ak.at[q, 1 + d], core)

    def ag_k(q):
        h, p = divmod(q, 2)
        for m in (2 * p, 2 * p + 1):
            blk = X.at[h, zls[m], (x + 2) % 4, k]
            arrived(blk, af.at[h, m], saf.at[h, m])
        col = X.at[h, planes(q), (x + 2) % 4, k]
        send(col, col, sak.at[q, 3], ak.at[q, 3], core)

    def ag_done(q):
        for i, xx in enumerate((x, (x + 3) % 4, (x + 1) % 4, (x + 2) % 4)):
            col = X.at[q // 2, planes(q), xx, 1 - k]
            arrived(col, ak.at[q, i], sak.at[q, i])

    def cols(j):
        return pl.ds(j * F, F)

    def side(j, a):
        return pl.ds(j * F + a * F2, F2)

    def m1(u):
        q, j = divmod(u, J)
        part = dot_nn(X[q // 2, planes(q)].reshape(256, WIDTH), W[:, cols(j)])
        PH[q, :, :, cols(j)] = part.astype(BF).reshape(4, 64, F)
        for i, d, near, a in ((0, 0, 2, 0), (1, 1, 2, 1), (2, 0, 1, 1), (3, 1, 3, 0)):
            buf = RA if i < 2 else RB
            send(
                PH.at[q, (y + near) % 4, :, side(j, a)], buf.at[q, :, side(j, a)],
                sry.at[u, i], ry.at[u, i], ypeer[d],
            )

    def r1(u):
        q, j = divmod(u, J)
        for a in range(2):
            sl = side(j, a)
            arrived(RA.at[q, :, sl], ry.at[u, a], sry.at[u, a])
            CB[q, :, sl] = (
                PH[q, (y + 1 + 2 * a) % 4, :, sl].astype(F32) + RA[q, :, sl].astype(F32)
            ).astype(BF)
            send(CB.at[q, :, sl], RC.at[q, :, sl], sry.at[u, 4 + a], ry.at[u, 4 + a], ypeer[a])

    def r2(u):
        q, j = divmod(u, J)
        js = cols(j)
        for i, buf, a in ((2, RB, 1), (3, RB, 0), (4, RC, 0), (5, RC, 1)):
            arrived(buf.at[q, :, side(j, a)], ry.at[u, i], sry.at[u, i])
        total = PH[q, y, :, js].astype(F32) + RB[q, :, js].astype(F32) + RC[q, :, js].astype(F32)

        @pl.when(owner[q])
        def _():
            OWN[q, :, js] = total

        @pl.when(other[q])
        def _():
            ZS[q, :, js] = total.astype(BF)
            remote(ZS.at[q, :, js], ZR.at[q, :, js], srz.at[u], rz.at[u], zpart).start()

    def share(u, yy):
        q, j = divmod(u, J)
        return COT.at[q // 2, ss[q] * 4 + yy, :, cols(j)]

    def give(u):
        for d in range(2):
            blk = share(u, y)
            remote(blk, blk, sgy.at[u, d], gy.at[u, d], ypeer[d]).start()

    def go(u):
        q, j = divmod(u, J)
        h, js = q // 2, cols(j)

        @pl.when(owner[q])
        def _():
            arrived(ZR.at[q, :, js], rz.at[u], srz.at[u])
            bias = jnp.concatenate(
                [bias_ref[pl.ds(j * (F // 128) + i, 1), :] for i in range(F // 128)], axis=1
            )
            v = OWN[q, :, js] + ZR[q, :, js].astype(F32) + bias
            sq = v * v
            t = jnp.tanh(gelu_const * v * (1.0 + 0.044715 * sq))
            half = 0.5 * (1.0 + t)
            slope = half + 0.5 * v * (1.0 - t * t) * gelu_const * (1.0 + 3.0 * 0.044715 * sq)
            ct = CT[:, h, :, js].reshape(64, F).astype(F32)
            COT[h, r, :, js] = (ct * slope).astype(BF)
            blk = share(u, y)
            remote(blk, blk, sgz.at[u], gz.at[u], zpart).start()
            give(u)
            ACT[:, h, :, js] = (v * half).astype(BF).reshape(4, 16, F)

    def gn(u):
        @pl.when(other[u // J])
        def _():
            arrived(share(u, y), gz.at[u], sgz.at[u])
            give(u)

    def fw(u):
        q, j = divmod(u, J)
        for d in range(2):
            yy = (y + 3 - 2 * d) % 4
            arrived(share(u, yy), gy.at[u, d], sgy.at[u, d])
            blk = COT.at[q // 2, ss[q] * 4 + yy, :, side(j, d)]
            remote(blk, blk, sgf.at[u, d], gf.at[u, d], ypeer[d]).start()

    def fo(u):
        @pl.when(owner[u // J])
        def _():
            fw(u)

    def fn(u):
        @pl.when(other[u // J])
        def _():
            fw(u)

    def gd(u):
        q, j = divmod(u, J)
        for d in range(2):
            blk = COT.at[q // 2, ss[q] * 4 + (y + 2) % 4, :, side(j, d)]
            arrived(blk, gf.at[u, d], sgf.at[u, d])

    def feats(q, n):
        w = WIDTH // NS[q]
        return pl.ds(n * w, w)

    def m3(q, n):
        w = WIDTH // NS[q]
        step = 512 if w % 512 == 0 else w
        cot = COT[q // 2, pl.ds(4 * ss[q], 4)].reshape(256, WIDTH)
        for i in range(w // step):
            sl = pl.ds(n * w + i * step, step)
            IGB[q, :, :, :, :, sl] = dot_nt(cot, W[sl, :]).astype(BF).reshape(2, 4, 2, 16, step)
        ns = feats(q, n)
        send(IGB.at[q, :, :, 1 - k, :, ns], RK.at[q, :, :, :, ns], sck.at[q, n], ck.at[q, n], core)

    def k1(q, n):
        ns = feats(q, n)
        arrived(RK.at[q, :, :, :, ns], ck.at[q, n], sck.at[q, n])
        S[q, :, :, :, ns] = (
            IGB[q, :, :, k, :, ns].astype(F32) + RK[q, :, :, :, ns].astype(F32)
        ).astype(BF)
        for i, d, near, a in ((0, 0, 2, 0), (1, 1, 2, 1), (2, 0, 1, 1), (3, 1, 3, 0)):
            buf = XA if i < 2 else XB
            send(
                S.at[q, a, (x + near) % 4, :, ns], buf.at[q, a, :, ns],
                scx.at[q, n, i], cx.at[q, n, i], xpeer[d],
            )

    def k2(q, n):
        ns = feats(q, n)
        for a in range(2):
            arrived(XA.at[q, a, :, ns], cx.at[q, n, a], scx.at[q, n, a])
            XM[q, a, :, ns] = (
                S[q, a, (x + 1 + 2 * a) % 4, :, ns].astype(F32) + XA[q, a, :, ns].astype(F32)
            ).astype(BF)
            send(XM.at[q, a, :, ns], XC.at[q, a, :, ns], scx.at[q, n, 4 + a], cx.at[q, n, 4 + a], xpeer[a])

    def k3(q, n):
        h, p = divmod(q, 2)
        ns = feats(q, n)
        for i, buf, a in ((2, XB, 1), (3, XB, 0), (4, XC, 0), (5, XC, 1)):
            arrived(buf.at[q, a, :, ns], cx.at[q, n, i], scx.at[q, n, i])
        T[q, :, :, ns] = (
            S[q, :, x, :, ns].astype(F32) + XB[q, :, :, ns].astype(F32) + XC[q, :, :, ns].astype(F32)
        ).astype(BF)
        for m in ((1,), (2, 3))[p]:
            send(
                T.at[q, zls[m] % 2, :, ns], ZT.at[h, m - 1, :, ns],
                scz.at[h, m - 1, n], cz.at[h, m - 1, n], zpeer[m],
            )

    def k4(h):
        for m in (1, 2, 3):
            q = 2 * h + (m > 1)
            for n in range(NS[q]):
                ns = feats(q, n)
                arrived(ZT.at[h, m - 1, :, ns], cz.at[h, m - 1, n], scz.at[h, m - 1, n])
        total = T[2 * h, zl % 2].astype(F32)
        for m in (1, 2, 3):
            total = total + ZT[h, m - 1].astype(F32)
        ig_ref[h] = total.astype(BF)

    def third(m):
        return pl.ds(m * 512, 512)

    def m2(m, j):
        a = X[:, :, :, :, :, third(m)].reshape(1024, 512)
        b = COT[:, :, :, third(j)].reshape(1024, 512)
        WG[third(m), third(j)] = dot_tn(a, b).astype(BF)

    def wg_copy(m):
        return pltpu.make_async_copy(WG.at[third(m)], wg_hbm.at[third(m)], wgsem.at[m])

    def m2_out(m):
        wg_copy(m).start()

    def act_copy():
        return pltpu.make_async_copy(ACT, act_hbm, actsem.at[0])

    def act_out():
        act_copy().start()

    def bg(j):
        w = WIDTH // 2
        total = jnp.sum(COT[:, :, :, pl.ds(j * w, w)].astype(F32).reshape(1024, w), axis=0, keepdims=True)
        for i in range(w // 128):
            bg_ref[pl.ds(j * (w // 128) + i, 1), :] = total[:, i * 128 : (i + 1) * 128]

    stages = dict(
        ag_start=ag_start, ag_z=ag_z, ag_f=ag_f, ag_k=ag_k, ag_done=ag_done, wload=wload,
        m1=m1, r1=r1, r2=r2, go=go, gn=gn, fo=fo, fn=fn, gd=gd,
        m3=m3, k1=k1, k2=k2, k3=k3, k4=k4, m2=m2, m2_out=m2_out, bg=bg, act_out=act_out,
    )
    for name, *args in ORDER:
        stages[name](*args)

    for copy in started:
        copy.wait_send()
    for u in range(UNITS):
        q, j = divmod(u, J)
        js = cols(j)

        @pl.when(other[q])
        def _():
            remote(ZS.at[q, :, js], ZR.at[q, :, js], srz.at[u], rz.at[u], zpart).wait_send()

        @pl.when(owner[q])
        def _():
            remote(share(u, y), share(u, y), sgz.at[u], gz.at[u], zpart).wait_send()

        for d in range(2):
            remote(share(u, y), share(u, y), sgy.at[u, d], gy.at[u, d], ypeer[d]).wait_send()
            blk = COT.at[q // 2, ss[q] * 4 + (y + 3 - 2 * d) % 4, :, side(j, d)]
            remote(blk, blk, sgf.at[u, d], gf.at[u, d], ypeer[d]).wait_send()
    act_copy().wait()
    for m in range(3):
        wg_copy(m).wait()


def hand_out(*refs):
    srcs, dsts, bufs, sems = refs[:4], refs[4:8], refs[8:12], refs[12]
    pieces = []
    for src, buf, dst in zip(srcs, bufs, dsts):
        parts = 8 if src.shape[0] == WIDTH else 1
        rows = src.shape[0] // parts
        pieces += [tuple(v.at[pl.ds(p * rows, rows)] for v in (src, buf, dst)) for p in range(parts)]
    ins = [pltpu.make_async_copy(s, b, sems.at[0, i]) for i, (s, b, _) in enumerate(pieces)]
    outs = [pltpu.make_async_copy(b, d, sems.at[1, i]) for i, (_, b, d) in enumerate(pieces)]
    for cp in ins:
        cp.start()
    for i, o in zip(ins, outs):
        i.wait()
        o.start()
    for o in outs:
        o.wait()


def local(inputs, weight, hidden_bias, act_cotangent):
    dma = pltpu.SemaphoreType.DMA
    sems = [
        (2, 3), (2, 2, 4), (2, 4), (Q, 4),
        (UNITS, 6), (UNITS,), (UNITS,), (UNITS, 2), (UNITS, 2),
        (Q, NMAX), (Q, NMAX, 6), (2, 3, NMAX),
    ]
    scratch = [
        pltpu.VMEM((2, 4, 4, 2, 16, WIDTH), BF),
        pltpu.VMEM((WIDTH, WIDTH), BF),
        pltpu.VMEM((4, 2, 16, WIDTH), BF),
        pltpu.VMEM((4, 2, 16, WIDTH), BF),
        pltpu.VMEM((Q, 4, 64, WIDTH), BF),
        pltpu.VMEM((Q, 64, WIDTH), BF),
        pltpu.VMEM((Q, 64, WIDTH), BF),
        pltpu.VMEM((Q, 64, WIDTH), BF),
        pltpu.VMEM((Q, 64, WIDTH), BF),
        pltpu.VMEM((Q, 64, WIDTH), BF),
        pltpu.VMEM((Q, 64, WIDTH), BF),
        pltpu.VMEM((Q, 64, WIDTH), F32),
        pltpu.VMEM((2, 8, 64, WIDTH), BF),
        pltpu.VMEM((Q, 2, 4, 2, 16, WIDTH), BF),
        pltpu.VMEM((Q, 2, 4, 16, WIDTH), BF),
        pltpu.VMEM((Q, 2, 4, 16, WIDTH), BF),
        pltpu.VMEM((Q, 2, 16, WIDTH), BF),
        pltpu.VMEM((Q, 2, 16, WIDTH), BF),
        pltpu.VMEM((Q, 2, 16, WIDTH), BF),
        pltpu.VMEM((Q, 2, 16, WIDTH), BF),
        pltpu.VMEM((Q, 2, 16, WIDTH), BF),
        pltpu.VMEM((2, 3, 16, WIDTH), BF),
        pltpu.VMEM((WIDTH, WIDTH), BF),
        dma((4,)), dma((3,)), dma((1,)),
    ] + [dma(s) for s in sems + sems]
    hbm = pl.BlockSpec(memory_space=pl.ANY)
    vmem = pl.BlockSpec(memory_space=pltpu.VMEM)
    shapes = (
        jax.ShapeDtypeStruct((4, 2, 16, WIDTH), BF),
        jax.ShapeDtypeStruct((2, 16, WIDTH), BF),
        jax.ShapeDtypeStruct((WIDTH, WIDTH), BF),
        jax.ShapeDtypeStruct((WIDTH // 128, 128), F32),
    )
    results = pl.pallas_call(
        kernel,
        out_shape=shapes,
        in_specs=[hbm, hbm, vmem, hbm],
        out_specs=(hbm, vmem, hbm, vmem),
        scratch_shapes=scratch,
        compiler_params=pltpu.CompilerParams(
            collective_id=0, has_side_effects=True, vmem_limit_bytes=56 << 20
        ),
        name="ffn",
    )(
        inputs.reshape(2, 16, WIDTH),
        weight,
        hidden_bias.reshape(WIDTH // 128, 128),
        act_cotangent.reshape(4, 2, 16, WIDTH),
    )
    act, ig, wg, bgr = pl.pallas_call(
        hand_out,
        out_shape=shapes,
        in_specs=[hbm] * 4,
        out_specs=(hbm,) * 4,
        scratch_shapes=[pltpu.VMEM(v.shape, v.dtype) for v in shapes] + [dma((2, 11))],
        compiler_params=pltpu.CompilerParams(vmem_limit_bytes=56 << 20),
        name="hand_out",
    )(*results)
    return act.reshape(128, WIDTH), ig.reshape(32, WIDTH), wg, bgr.reshape(WIDTH)


def solution(mesh):
    in_specs = (P("col", "row"), P("row", "col"), P("col"), P("row", "col"))
    out_specs = (P("row", "col"), P("col", "row"), P("row", "col"), P("col"))
    return jax.shard_map(local, mesh=mesh, in_specs=in_specs, out_specs=out_specs, check_vma=False)
```

```python
import math

import jax
import jax.numpy as jnp
from jax import lax
from jax.experimental import pallas as pl
from jax.experimental.pallas import tpu as pltpu
from jax.sharding import PartitionSpec as P

gelu_const = math.sqrt(2.0 / math.pi)
BF = jnp.bfloat16
F32 = jnp.float32
MESH = pl.DeviceIdType.MESH

WIDTH = 1536
Q = 4
J = 2
F = WIDTH // J
F2 = F // 2
UNITS = Q * J
NS = (1, 1, 1, 2)
NMAX = max(NS)


def dot_nn(a, b):
    return lax.dot_general(a, b, (((1,), (0,)), ((), ())), preferred_element_type=F32)


def dot_nt(a, b):
    return lax.dot_general(a, b, (((1,), (1,)), ((), ())), preferred_element_type=F32)


def dot_tn(a, b):
    return lax.dot_general(a, b, (((0,), (0,)), ((), ())), preferred_element_type=F32)


ORDER = (
    ("ag_start", 0), ("ag_start", 1), ("ag_z", 0), ("ag_z", 1), ("ag_f", 0), ("ag_z", 2), ("ag_f", 1),
    ("ag_k", 0), ("ag_z", 3), ("ag_done", 0), ("wload",), ("m1", 0), ("ag_k", 1), ("m1", 1),
    ("ag_done", 1), ("m1", 3), ("ag_f", 3), ("ag_f", 2), ("r1", 1), ("r1", 3), ("m1", 2),
    ("ag_k", 2), ("ag_k", 3), ("r2", 1), ("r1", 0), ("r2", 3), ("ag_done", 2), ("r1", 2),
    ("m1", 5), ("r2", 0), ("m1", 4), ("r2", 2), ("ag_done", 3), ("m1", 6), ("r1", 5),
    ("r1", 4), ("go", 3), ("go", 1), ("r1", 6), ("m1", 7), ("r2", 5), ("go", 0),
    ("r2", 4), ("r2", 6), ("r1", 7), ("fo", 0), ("go", 2), ("gn", 1), ("fo", 3),
    ("fo", 1), ("gn", 0), ("fn", 1), ("r2", 7), ("go", 6), ("fn", 0), ("gn", 3),
    ("go", 5), ("go", 7), ("go", 4), ("act_out",), ("gd", 0), ("gn", 2), ("fo", 6),
    ("gd", 1), ("gn", 5), ("fn", 3), ("m3", 0, 0), ("fo", 2), ("fn", 2), ("fo", 4),
    ("gd", 3), ("gn", 4), ("gn", 6), ("fn", 5), ("fo", 5), ("gd", 2), ("k1", 0, 0),
    ("gn", 7), ("m3", 1, 0), ("fn", 4), ("fn", 6), ("k2", 0, 0), ("k1", 1, 0), ("fn", 7),
    ("fo", 7), ("gd", 5), ("gd", 4), ("m3", 2, 0), ("gd", 6), ("k2", 1, 0), ("gd", 7),
    ("m3", 3, 0), ("k1", 2, 0), ("m3", 3, 1), ("k3", 0, 0), ("k1", 3, 0), ("m2", 2, 0), ("k1", 3, 1),
    ("bg", 1), ("k2", 2, 0), ("k3", 1, 0), ("k2", 3, 0), ("m2", 1, 1), ("k2", 3, 1), ("bg", 0),
    ("m2", 2, 2), ("k3", 2, 0), ("k3", 3, 0), ("m2", 1, 2), ("k3", 3, 1), ("k4", 0), ("m2", 2, 1),
    ("m2_out", 2), ("m2", 0, 1), ("m2", 0, 2), ("m2", 1, 0), ("m2_out", 1), ("m2", 0, 0), ("m2_out", 0),
    ("k4", 1),
)


def kernel(
    x_hbm, w_hbm, bias_ref, ct_hbm,
    act_hbm, ig_ref, wg_hbm, bg_ref,
    X, W, CT, ACT, PH, RA, RB, RC, CB, ZS, ZR, OWN, COT,
    IGB, RK, S, XA, XB, XC, XM, T, ZT, WG,
    loc, wgsem, actsem,
    az, ax, af, ak, ry, rz, gz, gy, gf, ck, cx, cz,
    saz, sax, saf, sak, sry, srz, sgz, sgy, sgf, sck, scx, scz,
):
    r = lax.axis_index("row")
    c = lax.axis_index("col")
    zh, y = r // 4, r % 4
    zl, x, k = c // 8, (c // 2) % 4, c % 2

    yp = (zh * 4 + (y + 1) % 4, c)
    ym = (zh * 4 + (y + 3) % 4, c)
    ypeer = (yp, ym)
    zpart = ((1 - zh) * 4 + y, c)
    xp = (r, zl * 8 + ((x + 1) % 4) * 2 + k)
    xm = (r, zl * 8 + ((x + 3) % 4) * 2 + k)
    xpeer = (xp, xm)
    core = (r, zl * 8 + x * 2 + (1 - k))
    zls = [zl, zl + 1 - 2 * (zl % 2), (zl + 2) % 4, 3 - zl]
    zpeer = [None] + [(r, zls[m] * 8 + x * 2 + k) for m in (1, 2, 3)]

    ss = [zl // 2, 1 - zl // 2] * 2
    owner = [zh == ss[q] for q in range(Q)]
    other = [zh != ss[q] for q in range(Q)]

    started = []

    def remote(src, dst, ssem, rsem, dev):
        return pltpu.make_async_remote_copy(
            src_ref=src, dst_ref=dst, send_sem=ssem, recv_sem=rsem, device_id=dev, device_id_type=MESH
        )

    def send(*args):
        copy = remote(*args)
        copy.start()
        started.append(copy)

    def arrived(dst, rsem, ssem):
        remote(dst, dst, ssem, rsem, core).wait_recv()

    cp_x = [pltpu.make_async_copy(x_hbm.at[h], X.at[h, zl, x, k], loc.at[h]) for h in range(2)]
    cp_w = pltpu.make_async_copy(w_hbm, W, loc.at[2])
    cp_ct = pltpu.make_async_copy(ct_hbm, CT, loc.at[3])
    for cp in cp_x:
        cp.start()
    cp_w.start()
    cp_ct.start()
    barrier = pltpu.get_barrier_semaphore()
    peers = [yp, ym, zpart, xp, xm, core] + zpeer[1:]
    for p in peers:
        pl.semaphore_signal(barrier, inc=1, device_id=p, device_id_type=MESH)
    pl.semaphore_wait(barrier, len(peers))
    for cp in cp_x:
        cp.wait()

    def wload():
        cp_w.wait()
        cp_ct.wait()

    def ag_start(h):
        own = X.at[h, zl, x, k]
        send(own, own, saz.at[h, 0], az.at[h, 0], zpeer[1])
        for d in range(2):
            send(own, own, sax.at[h, d, 0], ax.at[h, d, 0], xpeer[d])
        for m in (2, 3):
            send(own, own, saz.at[h, m - 1], az.at[h, m - 1], zpeer[m])

    def planes(q):
        return pl.ds(2 * ss[q], 2)

    def ag_z(q):
        h, p = divmod(q, 2)
        for m in ((1,), (2, 3))[p]:
            blk = X.at[h, zls[m], x, k]
            arrived(blk, az.at[h, m - 1], saz.at[h, m - 1])
            for d in range(2):
                send(blk, blk, sax.at[h, d, m], ax.at[h, d, m], xpeer[d])
        col = X.at[h, planes(q), x, k]
        send(col, col, sak.at[q, 0], ak.at[q, 0], core)

    def ag_f(q):
        h, p = divmod(q, 2)
        for m in (2 * p, 2 * p + 1):
            for d in (m % 2, 1 - m % 2):
                blk = X.at[h, zls[m], (x + 3 - 2 * d) % 4, k]
                arrived(blk, ax.at[h, d, m], sax.at[h, d, m])
                if d == m % 2:
                    send(blk, blk, saf.at[h, m], af.at[h, m], xpeer[d])
        for d in range(2):
            col = X.at[h, planes(q), (x + 3 - 2 * d) % 4, k]
            send(col, col, sak.at[q, 1 + d], ak.at[q, 1 + d], core)

    def ag_k(q):
        h, p = divmod(q, 2)
        for m in (2 * p, 2 * p + 1):
            blk = X.at[h, zls[m], (x + 2) % 4, k]
            arrived(blk, af.at[h, m], saf.at[h, m])
        col = X.at[h, planes(q), (x + 2) % 4, k]
        send(col, col, sak.at[q, 3], ak.at[q, 3], core)

    def ag_done(q):
        for i, xx in enumerate((x, (x + 3) % 4, (x + 1) % 4, (x + 2) % 4)):
            col = X.at[q // 2, planes(q), xx, 1 - k]
            arrived(col, ak.at[q, i], sak.at[q, i])

    def cols(j):
        return pl.ds(j * F, F)

    def side(j, a):
        return pl.ds(j * F + a * F2, F2)

    def m1(u):
        q, j = divmod(u, J)
        part = dot_nn(X[q // 2, planes(q)].reshape(256, WIDTH), W[:, cols(j)])
        PH[q, :, :, cols(j)] = part.astype(BF).reshape(4, 64, F)
        for i, d, near, a in ((0, 0, 2, 0), (1, 1, 2, 1), (2, 0, 1, 1), (3, 1, 3, 0)):
            buf = RA if i < 2 else RB
            send(
                PH.at[q, (y + near) % 4, :, side(j, a)], buf.at[q, :, side(j, a)],
                sry.at[u, i], ry.at[u, i], ypeer[d],
            )

    def r1(u):
        q, j = divmod(u, J)
        for a in range(2):
            sl = side(j, a)
            arrived(RA.at[q, :, sl], ry.at[u, a], sry.at[u, a])
            CB[q, :, sl] = (
                PH[q, (y + 1 + 2 * a) % 4, :, sl].astype(F32) + RA[q, :, sl].astype(F32)
            ).astype(BF)
            send(CB.at[q, :, sl], RC.at[q, :, sl], sry.at[u, 4 + a], ry.at[u, 4 + a], ypeer[a])

    def r2(u):
        q, j = divmod(u, J)
        js = cols(j)
        for i, buf, a in ((2, RB, 1), (3, RB, 0), (4, RC, 0), (5, RC, 1)):
            arrived(buf.at[q, :, side(j, a)], ry.at[u, i], sry.at[u, i])
        total = PH[q, y, :, js].astype(F32) + RB[q, :, js].astype(F32) + RC[q, :, js].astype(F32)

        @pl.when(owner[q])
        def _():
            OWN[q, :, js] = total

        @pl.when(other[q])
        def _():
            ZS[q, :, js] = total.astype(BF)
            remote(ZS.at[q, :, js], ZR.at[q, :, js], srz.at[u], rz.at[u], zpart).start()

    def share(u, yy):
        q, j = divmod(u, J)
        return COT.at[q // 2, ss[q] * 4 + yy, :, cols(j)]

    def give(u):
        for d in range(2):
            blk = share(u, y)
            remote(blk, blk, sgy.at[u, d], gy.at[u, d], ypeer[d]).start()

    def go(u):
        q, j = divmod(u, J)
        h, js = q // 2, cols(j)

        @pl.when(owner[q])
        def _():
            arrived(ZR.at[q, :, js], rz.at[u], srz.at[u])
            bias = jnp.concatenate(
                [bias_ref[pl.ds(j * (F // 128) + i, 1), :] for i in range(F // 128)], axis=1
            )
            v = OWN[q, :, js] + ZR[q, :, js].astype(F32) + bias
            sq = v * v
            t = jnp.tanh(gelu_const * v * (1.0 + 0.044715 * sq))
            half = 0.5 * (1.0 + t)
            slope = half + 0.5 * v * (1.0 - t * t) * gelu_const * (1.0 + 3.0 * 0.044715 * sq)
            ct = CT[:, h, :, js].reshape(64, F).astype(F32)
            COT[h, r, :, js] = (ct * slope).astype(BF)
            blk = share(u, y)
            remote(blk, blk, sgz.at[u], gz.at[u], zpart).start()
            give(u)
            ACT[:, h, :, js] = (v * half).astype(BF).reshape(4, 16, F)

    def gn(u):
        @pl.when(other[u // J])
        def _():
            arrived(share(u, y), gz.at[u], sgz.at[u])
            give(u)

    def fw(u):
        q, j = divmod(u, J)
        for d in range(2):
            yy = (y + 3 - 2 * d) % 4
            arrived(share(u, yy), gy.at[u, d], sgy.at[u, d])
            blk = COT.at[q // 2, ss[q] * 4 + yy, :, side(j, d)]
            remote(blk, blk, sgf.at[u, d], gf.at[u, d], ypeer[d]).start()

    def fo(u):
        @pl.when(owner[u // J])
        def _():
            fw(u)

    def fn(u):
        @pl.when(other[u // J])
        def _():
            fw(u)

    def gd(u):
        q, j = divmod(u, J)
        for d in range(2):
            blk = COT.at[q // 2, ss[q] * 4 + (y + 2) % 4, :, side(j, d)]
            arrived(blk, gf.at[u, d], sgf.at[u, d])

    def feats(q, n):
        w = WIDTH // NS[q]
        return pl.ds(n * w, w)

    def m3(q, n):
        w = WIDTH // NS[q]
        step = 512 if w % 512 == 0 else w
        cot = COT[q // 2, pl.ds(4 * ss[q], 4)].reshape(256, WIDTH)
        for i in range(w // step):
            sl = pl.ds(n * w + i * step, step)
            IGB[q, :, :, :, :, sl] = dot_nt(cot, W[sl, :]).astype(BF).reshape(2, 4, 2, 16, step)
        ns = feats(q, n)
        send(IGB.at[q, :, :, 1 - k, :, ns], RK.at[q, :, :, :, ns], sck.at[q, n], ck.at[q, n], core)

    def k1(q, n):
        ns = feats(q, n)
        arrived(RK.at[q, :, :, :, ns], ck.at[q, n], sck.at[q, n])
        S[q, :, :, :, ns] = (
            IGB[q, :, :, k, :, ns].astype(F32) + RK[q, :, :, :, ns].astype(F32)
        ).astype(BF)
        for i, d, near, a in ((0, 0, 2, 0), (1, 1, 2, 1), (2, 0, 1, 1), (3, 1, 3, 0)):
            buf = XA if i < 2 else XB
            send(
                S.at[q, a, (x + near) % 4, :, ns], buf.at[q, a, :, ns],
                scx.at[q, n, i], cx.at[q, n, i], xpeer[d],
            )

    def k2(q, n):
        ns = feats(q, n)
        for a in range(2):
            arrived(XA.at[q, a, :, ns], cx.at[q, n, a], scx.at[q, n, a])
            XM[q, a, :, ns] = (
                S[q, a, (x + 1 + 2 * a) % 4, :, ns].astype(F32) + XA[q, a, :, ns].astype(F32)
            ).astype(BF)
            send(XM.at[q, a, :, ns], XC.at[q, a, :, ns], scx.at[q, n, 4 + a], cx.at[q, n, 4 + a], xpeer[a])

    def k3(q, n):
        h, p = divmod(q, 2)
        ns = feats(q, n)
        for i, buf, a in ((2, XB, 1), (3, XB, 0), (4, XC, 0), (5, XC, 1)):
            arrived(buf.at[q, a, :, ns], cx.at[q, n, i], scx.at[q, n, i])
        T[q, :, :, ns] = (
            S[q, :, x, :, ns].astype(F32) + XB[q, :, :, ns].astype(F32) + XC[q, :, :, ns].astype(F32)
        ).astype(BF)
        for m in ((1,), (2, 3))[p]:
            send(
                T.at[q, zls[m] % 2, :, ns], ZT.at[h, m - 1, :, ns],
                scz.at[h, m - 1, n], cz.at[h, m - 1, n], zpeer[m],
            )

    def k4(h):
        for m in (1, 2, 3):
            q = 2 * h + (m > 1)
            for n in range(NS[q]):
                ns = feats(q, n)
                arrived(ZT.at[h, m - 1, :, ns], cz.at[h, m - 1, n], scz.at[h, m - 1, n])
        total = T[2 * h, zl % 2].astype(F32)
        for m in (1, 2, 3):
            total = total + ZT[h, m - 1].astype(F32)
        ig_ref[h] = total.astype(BF)

    def third(m):
        return pl.ds(m * 512, 512)

    def m2(m, j):
        a = X[:, :, :, :, :, third(m)].reshape(1024, 512)
        b = COT[:, :, :, third(j)].reshape(1024, 512)
        WG[third(m), third(j)] = dot_tn(a, b).astype(BF)

    def wg_copy(m):
        return pltpu.make_async_copy(WG.at[third(m)], wg_hbm.at[third(m)], wgsem.at[m])

    def m2_out(m):
        wg_copy(m).start()

    def act_copy():
        return pltpu.make_async_copy(ACT, act_hbm, actsem.at[0])

    def act_out():
        act_copy().start()

    def bg(j):
        w = WIDTH // 2
        total = jnp.sum(COT[:, :, :, pl.ds(j * w, w)].astype(F32).reshape(1024, w), axis=0, keepdims=True)
        for i in range(w // 128):
            bg_ref[pl.ds(j * (w // 128) + i, 1), :] = total[:, i * 128 : (i + 1) * 128]

    stages = dict(
        ag_start=ag_start, ag_z=ag_z, ag_f=ag_f, ag_k=ag_k, ag_done=ag_done, wload=wload,
        m1=m1, r1=r1, r2=r2, go=go, gn=gn, fo=fo, fn=fn, gd=gd,
        m3=m3, k1=k1, k2=k2, k3=k3, k4=k4, m2=m2, m2_out=m2_out, bg=bg, act_out=act_out,
    )
    for name, *args in ORDER:
        stages[name](*args)

    for copy in started:
        copy.wait_send()
    for u in range(UNITS):
        q, j = divmod(u, J)
        js = cols(j)

        @pl.when(other[q])
        def _():
            remote(ZS.at[q, :, js], ZR.at[q, :, js], srz.at[u], rz.at[u], zpart).wait_send()

        @pl.when(owner[q])
        def _():
            remote(share(u, y), share(u, y), sgz.at[u], gz.at[u], zpart).wait_send()

        for d in range(2):
            remote(share(u, y), share(u, y), sgy.at[u, d], gy.at[u, d], ypeer[d]).wait_send()
            blk = COT.at[q // 2, ss[q] * 4 + (y + 3 - 2 * d) % 4, :, side(j, d)]
            remote(blk, blk, sgf.at[u, d], gf.at[u, d], ypeer[d]).wait_send()
    act_copy().wait()
    for m in range(3):
        wg_copy(m).wait()


def hand_out(*refs):
    srcs, dsts, bufs, sems = refs[:4], refs[4:8], refs[8:12], refs[12]
    pieces = []
    for src, buf, dst in zip(srcs, bufs, dsts):
        parts = 8 if src.shape[0] == WIDTH else 1
        rows = src.shape[0] // parts
        pieces += [tuple(v.at[pl.ds(p * rows, rows)] for v in (src, buf, dst)) for p in range(parts)]
    ins = [pltpu.make_async_copy(s, b, sems.at[0, i]) for i, (s, b, _) in enumerate(pieces)]
    outs = [pltpu.make_async_copy(b, d, sems.at[1, i]) for i, (_, b, d) in enumerate(pieces)]
    for cp in ins:
        cp.start()
    for i, o in zip(ins, outs):
        i.wait()
        o.start()
    for o in outs:
        o.wait()


def local(inputs, weight, hidden_bias, act_cotangent):
    dma = pltpu.SemaphoreType.DMA
    sems = [
        (2, 3), (2, 2, 4), (2, 4), (Q, 4),
        (UNITS, 6), (UNITS,), (UNITS,), (UNITS, 2), (UNITS, 2),
        (Q, NMAX), (Q, NMAX, 6), (2, 3, NMAX),
    ]
    scratch = [
        pltpu.VMEM((2, 4, 4, 2, 16, WIDTH), BF),
        pltpu.VMEM((WIDTH, WIDTH), BF),
        pltpu.VMEM((4, 2, 16, WIDTH), BF),
        pltpu.VMEM((4, 2, 16, WIDTH), BF),
        pltpu.VMEM((Q, 4, 64, WIDTH), BF),
        pltpu.VMEM((Q, 64, WIDTH), BF),
        pltpu.VMEM((Q, 64, WIDTH), BF),
        pltpu.VMEM((Q, 64, WIDTH), BF),
        pltpu.VMEM((Q, 64, WIDTH), BF),
        pltpu.VMEM((Q, 64, WIDTH), BF),
        pltpu.VMEM((Q, 64, WIDTH), BF),
        pltpu.VMEM((Q, 64, WIDTH), F32),
        pltpu.VMEM((2, 8, 64, WIDTH), BF),
        pltpu.VMEM((Q, 2, 4, 2, 16, WIDTH), BF),
        pltpu.VMEM((Q, 2, 4, 16, WIDTH), BF),
        pltpu.VMEM((Q, 2, 4, 16, WIDTH), BF),
        pltpu.VMEM((Q, 2, 16, WIDTH), BF),
        pltpu.VMEM((Q, 2, 16, WIDTH), BF),
        pltpu.VMEM((Q, 2, 16, WIDTH), BF),
        pltpu.VMEM((Q, 2, 16, WIDTH), BF),
        pltpu.VMEM((Q, 2, 16, WIDTH), BF),
        pltpu.VMEM((2, 3, 16, WIDTH), BF),
        pltpu.VMEM((WIDTH, WIDTH), BF),
        dma((4,)), dma((3,)), dma((1,)),
    ] + [dma(s) for s in sems + sems]
    hbm = pl.BlockSpec(memory_space=pl.ANY)
    vmem = pl.BlockSpec(memory_space=pltpu.VMEM)
    shapes = (
        jax.ShapeDtypeStruct((4, 2, 16, WIDTH), BF),
        jax.ShapeDtypeStruct((2, 16, WIDTH), BF),
        jax.ShapeDtypeStruct((WIDTH, WIDTH), BF),
        jax.ShapeDtypeStruct((WIDTH // 128, 128), F32),
    )
    results = pl.pallas_call(
        kernel,
        out_shape=shapes,
        in_specs=[hbm, hbm, vmem, hbm],
        out_specs=(hbm, vmem, hbm, vmem),
        scratch_shapes=scratch,
        compiler_params=pltpu.CompilerParams(
            collective_id=0, has_side_effects=True, vmem_limit_bytes=56 << 20
        ),
        name="ffn",
    )(
        inputs.reshape(2, 16, WIDTH),
        weight,
        hidden_bias.reshape(WIDTH // 128, 128),
        act_cotangent.reshape(4, 2, 16, WIDTH),
    )
    act, ig, wg, bgr = pl.pallas_call(
        hand_out,
        out_shape=shapes,
        in_specs=[hbm] * 4,
        out_specs=(hbm,) * 4,
        scratch_shapes=[pltpu.VMEM(v.shape, v.dtype) for v in shapes] + [dma((2, 11))],
        compiler_params=pltpu.CompilerParams(vmem_limit_bytes=56 << 20),
        name="hand_out",
    )(*results)
    return act.reshape(128, WIDTH), ig.reshape(32, WIDTH), wg, bgr.reshape(WIDTH)


def solution(mesh):
    in_specs = (P("col", "row"), P("row", "col"), P("col"), P("row", "col"))
    out_specs = (P("row", "col"), P("col", "row"), P("row", "col"), P("col"))
    return jax.shard_map(local, mesh=mesh, in_specs=in_specs, out_specs=out_specs, check_vma=False)
```
